128 devices in a mesh: dp: 16 (over x, z_lo, core), center: 8 (over z_hi, y).
Axes of the slice: x: 4, y: 4, z: 4 (z_hi: 2, z_lo: 2; z = z_hi * 2 + z_lo), core: 2. Of those that a mesh axis runs over, the one named last changes fastest.
Arguments:
- points: bfloat16 [24576, 128], P('dp'), may hold values from -1.5 to 1.5, as said below
- centers: bfloat16 [65536, 128], P('center'), may hold values from -1.5 to 1.5, as said below
- direction: float32 [65536, 128], P('center'), may hold values from -4 to 4, as said below
Outputs:
- product: float32 [65536, 128], P('center')
The draws below stay inside these ranges and needn't reach their ends.
Inputs may be any that keep to these rules, and one draw needn't show every extreme that they name: Every row of points has a squared length of 128 up to bfloat16 rounding. Every row of centers has a squared length of 128 up to bfloat16 rounding. Every column of direction sums to zero.
All inputs are finite; a program needn't handle non-finite values.
Results may differ from the reference program's by a relative error of at most 0.003.
Values may be sent and summed in bfloat16 or wider, within the bound.
No kernel may reach another device: no remote copies, remote signals or barrier semaphores. Data moves between devices by JAX's collectives and lax.ppermute only.
A program may use at most 128 MiB of HBM per device.

```python
import math
import jax
import jax.numpy as jnp
from jax import lax

D = 128
P_SIZE = 128
CENTERS = 65536
POINTS = 24576


def on_circles(angles):
    radius = math.sqrt(2.0)
    return jnp.concatenate([radius * jnp.cos(angles), radius * jnp.sin(angles)], axis=1)


def draw_points(key, part):
    key = jax.random.fold_in(key, 11)
    angles = jax.random.uniform(key, (POINTS, D // 2), jnp.float32, -math.pi, math.pi)
    return on_circles(angles).astype(jnp.bfloat16)


def draw_centers(key, part):
    key = jax.random.fold_in(key, 12)
    angles = jax.random.uniform(key, (CENTERS, D // 2), jnp.float32, -math.pi, math.pi)
    return on_circles(angles).astype(jnp.bfloat16)


def draw_direction(key, part):
    key = jax.random.fold_in(key, 13)
    values = jnp.clip(jax.random.normal(key, (CENTERS // 2, P_SIZE), jnp.float32), -4.0, 4.0)
    return jnp.stack([values, -values], axis=1).reshape(CENTERS, P_SIZE)


def setup_inputs(seed: int = 0) -> dict:
    key_of = jax.random.split(jax.random.key(seed), 4)
    points = draw_points(jax.random.fold_in(key_of[3], 71), 0)
    centers = draw_centers(jax.random.fold_in(key_of[3], 71), 0)
    direction = draw_direction(jax.random.fold_in(key_of[3], 71), 0)
    return {"points": points, "centers": centers, "direction": direction}


width_scale = 6.4

def kernel_tile(pts, cens, cen_sq, gamma, amp):
    pts_sq = lax.optimization_barrier(jnp.sum(pts.astype(jnp.float32) ** 2, axis=1))
    cross = jnp.dot(pts, cens.T, preferred_element_type=jnp.float32)
    dist = pts_sq[:, None] + cen_sq[None, :] - 2.0 * cross
    return jnp.exp(amp - gamma * dist).astype(jnp.bfloat16)

def reference(points, centers, direction):
    gamma = width_scale / D
    amp = 0.5 * D * jnp.log1p(4.0 * width_scale / D)
    cen_sq = lax.optimization_barrier(jnp.sum(centers.astype(jnp.float32) ** 2, axis=1))
    dir_b = direction.astype(jnp.bfloat16)
    block = min(512, POINTS)
    blocks = points.reshape(POINTS // block, block, D)

    def step(total, pts):
        kernel = kernel_tile(pts, centers, cen_sq, gamma, amp)
        fitted = jnp.dot(kernel, dir_b, preferred_element_type=jnp.float32)
        fitted_b = (fitted / jnp.sqrt(jnp.float32(CENTERS))).astype(jnp.bfloat16)
        return (total + jnp.dot(kernel.T, fitted_b, preferred_element_type=jnp.float32), None)
    total, _ = lax.scan(step, jnp.zeros((CENTERS, P_SIZE), jnp.float32), blocks)
    return total / jnp.sqrt(jnp.float32(POINTS))
```

```python
import functools
import math

import jax
import jax.numpy as jnp
from jax import lax
from jax.experimental import pallas as pl
from jax.experimental.pallas import tpu as pltpu
from jax.sharding import PartitionSpec as P

CENTERS = 65536
POINTS = 24576
WIDTH = 128
GAMMA = 6.4 / WIDTH
AMP = 0.5 * WIDTH * math.log1p(4.0 * GAMMA)
LOG2E = math.log2(math.e)
CROSS_SCALE = 2.0 * GAMMA * LOG2E
BF16 = jnp.bfloat16
F32 = jnp.float32
ROWS_BY_ROWS = (((1,), (1,)), ((), ()))


def split_bf16(x):
    high = x.astype(BF16)
    return high, (x - high.astype(F32)).astype(BF16)


def row_squares(x):
    x = x.astype(F32)
    return jnp.sum(x * x, axis=1, keepdims=True)


def fit_kernel(tile_rows, points_ref, centers_ref, direction_ref, tile_ref, fit_ref, scaled_ref, sum_ref):
    step = pl.program_id(0)
    rows = points_ref.shape[0]
    cols = centers_ref.shape[0]

    @pl.when(step == 0)
    def _():
        high, low = split_bf16(points_ref[...].astype(F32) * CROSS_SCALE)
        scaled_ref[:, :WIDTH] = high
        scaled_ref[:, WIDTH:] = low
        sum_ref[...] = jnp.zeros_like(sum_ref)

    chunk = 1024
    for part in range(cols // chunk):
        here = slice(part * chunk, (part + 1) * chunk)
        cens = centers_ref[here, :]
        factor = jnp.exp2(-GAMMA * LOG2E * row_squares(cens))
        high, low = split_bf16(direction_ref[here, :].astype(BF16).astype(F32) * factor)
        weights = jnp.concatenate([high, low], axis=1)
        twice = jnp.concatenate([cens, cens], axis=1)
        for t in range(rows // tile_rows):
            at = slice(t * tile_rows, (t + 1) * tile_rows)
            cross = lax.dot_general(scaled_ref[at, :], twice, ROWS_BY_ROWS, preferred_element_type=F32)
            tile = jnp.exp2(cross).astype(BF16)
            tile_ref[at, pl.ds(pl.multiple_of(step * cols + part * chunk, chunk), chunk)] = tile
            sum_ref[at, :] += jnp.dot(tile, weights, preferred_element_type=F32)

    @pl.when(step == pl.num_programs(0) - 1)
    def _():
        factor = jnp.exp2(2.0 * LOG2E * (AMP - GAMMA * row_squares(points_ref[...])))
        factor = factor * (1.0 / math.sqrt(CENTERS))
        fit_ref[...] = (sum_ref[:, :WIDTH] + sum_ref[:, WIDTH:]) * factor


def fit_call(points, centers, direction, cols=2048, tile_rows=256):
    rows, count = points.shape[0], centers.shape[0]
    return pl.pallas_call(
        functools.partial(fit_kernel, tile_rows),
        grid=(count // cols,),
        in_specs=[
            pl.BlockSpec((rows, WIDTH), lambda j: (0, 0)),
            pl.BlockSpec((cols, WIDTH), lambda j: (j, 0)),
            pl.BlockSpec((cols, WIDTH), lambda j: (j, 0)),
        ],
        out_specs=[
            pl.BlockSpec(memory_space=pltpu.VMEM),
            pl.BlockSpec((rows, WIDTH), lambda j: (0, 0)),
        ],
        out_shape=[pltpu.VMEM((rows, count), BF16), jax.ShapeDtypeStruct((rows, WIDTH), F32)],
        scratch_shapes=[pltpu.VMEM((rows, 2 * WIDTH), BF16), pltpu.VMEM((rows, 2 * WIDTH), F32)],
        compiler_params=pltpu.CompilerParams(vmem_limit_bytes=30 * 2**20),
        name="fit_tiles",
    )(points, centers, direction)


def back_kernel(half_ref, fitted_ref, centers_ref, tile_ref, out_ref, turned_ref):
    step = pl.program_id(0)
    cols = centers_ref.shape[0]
    half = half_ref[0]
    span = cols * pl.num_programs(0)

    @pl.when(step == 0)
    def _():
        turned_ref[...] = fitted_ref[...].astype(F32).T.astype(BF16)

    factor = jnp.exp2(-GAMMA * LOG2E * row_squares(centers_ref[...])) * (1.0 / math.sqrt(POINTS))
    tile = tile_ref[:, pl.ds(pl.multiple_of(half * span + step * cols, cols), cols)]
    out = jnp.dot(turned_ref[...], tile, preferred_element_type=F32).T
    out_ref[...] = (out * factor).astype(BF16)


def back_call(half, fitted, centers, tiles, cols=2048):
    rows, count = tiles.shape
    steps = count // 2 // cols
    tiles = pltpu.with_memory_space_constraint(tiles, pltpu.VMEM)
    return pl.pallas_call(
        back_kernel,
        grid_spec=pltpu.PrefetchScalarGridSpec(
            num_scalar_prefetch=1,
            grid=(steps,),
            in_specs=[
                pl.BlockSpec((rows, WIDTH), lambda j, half: (0, 0)),
                pl.BlockSpec((cols, WIDTH), lambda j, half: (half[0] * steps + j, 0)),
                pl.BlockSpec(memory_space=pltpu.VMEM),
            ],
            out_specs=pl.BlockSpec((cols, WIDTH), lambda j, half: (j, 0)),
            scratch_shapes=[pltpu.VMEM((WIDTH, rows), BF16)],
        ),
        out_shape=jax.ShapeDtypeStruct((count // 2, WIDTH), BF16),
        compiler_params=pltpu.CompilerParams(vmem_limit_bytes=16 * 2**20),
        name="back_tiles",
    )(half, fitted, centers, tiles)


def widen_kernel(core_ref, mine_ref, other_ref, out_ref):
    mine = pl.program_id(0) == core_ref[0]

    @pl.when(mine)
    def _():
        out_ref[...] = mine_ref[...].astype(F32)

    @pl.when(jnp.logical_not(mine))
    def _():
        out_ref[...] = other_ref[...].astype(F32)


def widen_call(core, mine, other, block=2048):
    count = mine.shape[0]
    steps = count // block
    return pl.pallas_call(
        widen_kernel,
        grid_spec=pltpu.PrefetchScalarGridSpec(
            num_scalar_prefetch=1,
            grid=(2, steps),
            in_specs=[
                pl.BlockSpec((block, WIDTH), lambda h, j, core: (jnp.where(h == core[0], j, 0), 0)),
                pl.BlockSpec((block, WIDTH), lambda h, j, core: (jnp.where(h == core[0], 0, j), 0)),
            ],
            out_specs=pl.BlockSpec((block, WIDTH), lambda h, j, core: (h * steps + j, 0)),
        ),
        out_shape=jax.ShapeDtypeStruct((2 * count, WIDTH), F32),
        name="widen",
    )(core, mine, other)


def per_device(points, centers, direction):
    rows, count = points.shape[0], centers.shape[0]
    dp, groups = lax.axis_size("dp"), lax.axis_size("center")
    core = lax.rem(lax.axis_index("dp"), 2)
    chips = dp // 2
    same_core = [[2 * chip + c for chip in range(chips)] for c in range(2)]
    swap = [(i, i ^ 1) for i in range(dp)]

    tiles, partial_fit = fit_call(points, centers, direction)
    part = rows // groups
    pieces = lax.all_to_all(partial_fit.reshape(groups, part, WIDTH), "center", 0, 0)
    fitted = jnp.sum(pieces, axis=0).astype(BF16)
    fitted = jnp.broadcast_to(fitted[None], (groups, part, WIDTH))
    fitted = lax.all_to_all(fitted, "center", 0, 0).reshape(rows, WIDTH)

    mine_id = core.astype(jnp.int32).reshape(1)
    theirs = back_call(1 - mine_id, fitted, centers, tiles)
    received = lax.ppermute(theirs, "dp", swap)
    mine = back_call(mine_id, fitted, centers, tiles)
    both = (mine.astype(F32) + received.astype(F32)).astype(BF16)
    part = count // 2 // chips
    pieces = lax.all_to_all(
        both.reshape(chips, part, WIDTH), "dp", 0, 0, axis_index_groups=same_core
    )
    summed = jnp.sum(pieces.astype(F32), axis=0).astype(BF16)
    summed = jnp.broadcast_to(summed[None], (chips, part, WIDTH))
    summed = lax.all_to_all(summed, "dp", 0, 0, axis_index_groups=same_core)
    summed = summed.reshape(count // 2, WIDTH)
    other = lax.ppermute(summed, "dp", swap)
    return widen_call(mine_id, summed, other)


def solution(mesh):
    return jax.shard_map(
        per_device,
        mesh=mesh,
        in_specs=(P("dp", None), P("center", None), P("center", None)),
        out_specs=P("center", None),
        check_vma=False,
    )
```

```python
import functools
import math

import jax
import jax.numpy as jnp
from jax import lax
from jax.experimental import pallas as pl
from jax.experimental.pallas import tpu as pltpu
from jax.sharding import PartitionSpec as P

CENTERS = 65536
POINTS = 24576
WIDTH = 128
GAMMA = 6.4 / WIDTH
AMP = 0.5 * WIDTH * math.log1p(4.0 * GAMMA)
LOG2E = math.log2(math.e)
CROSS_SCALE = 2.0 * GAMMA * LOG2E
BF16 = jnp.bfloat16
F32 = jnp.float32
ROWS_BY_ROWS = (((1,), (1,)), ((), ()))


def split_bf16(x):
    high = x.astype(BF16)
    return high, (x - high.astype(F32)).astype(BF16)


def row_squares(x):
    x = x.astype(F32)
    return jnp.sum(x * x, axis=1, keepdims=True)


VMEM = pl.BlockSpec(memory_space=pltpu.VMEM)

OFFSETS = ((0, 2, 5, 7), (4, 1, 3, 6))
SETS = len(OFFSETS[0])
PACKED = [sum(k << (4 * j) for j, k in enumerate(row)) for row in OFFSETS]


def owner(me, j, other):
    table = jnp.where((me & 1) == other, PACKED[0], PACKED[1])
    return (me >> 1) ^ ((table >> (4 * j)) & 7)


def exchange(x, j):
    pairs = [
        (2 * chip + c, 2 * (chip ^ OFFSETS[c][j]) + c)
        for chip in range(8)
        for c in range(2)
        if OFFSETS[c][j]
    ]
    return lax.ppermute(x, "dp", pairs)


def on_chip(x):
    return pltpu.with_memory_space_constraint(x, pltpu.VMEM)


def in_hbm(x):
    return pltpu.with_memory_space_constraint(x, pltpu.HBM)


def fit_kernel(tile_rows, points_ref, centers_ref, direction_ref, tile_ref, fit_ref, scaled_ref, turned_ref, weights_ref, sum_ref):
    step = pl.program_id(0)
    rows = points_ref.shape[0]
    cols = centers_ref.shape[0]

    @pl.when(step == 0)
    def _():
        high, low = split_bf16(points_ref[...].astype(F32) * CROSS_SCALE)
        scaled_ref[:, :WIDTH] = high
        scaled_ref[:, WIDTH:] = low
        sum_ref[...] = jnp.zeros_like(sum_ref)

    turned = centers_ref[...].astype(F32).T
    shift = jnp.sum(turned * turned, axis=0, keepdims=True) * (-GAMMA * LOG2E)
    turned = turned.astype(BF16)
    turned_ref[:WIDTH, :] = turned
    turned_ref[WIDTH:, :] = turned
    weights_ref[...] = direction_ref[...].astype(BF16)

    def make(t):
        at = slice(t * tile_rows, (t + 1) * tile_rows)
        cross = jnp.dot(scaled_ref[at, :], turned_ref[...], preferred_element_type=F32)
        tile = jnp.exp2(cross + shift).astype(BF16)
        tile_ref[at, pl.ds(pl.multiple_of(step * cols, cols), cols)] = tile
        return tile

    def fit(t, tile):
        at = slice(t * tile_rows, (t + 1) * tile_rows)
        sum_ref[at, :] += jnp.dot(tile, weights_ref[...], preferred_element_type=F32)

    count = rows // tile_rows
    last = make(0)
    for t in range(1, count):
        tile = make(t)
        fit(t - 1, last)
        last = tile
    fit(count - 1, last)

    @pl.when(step == pl.num_programs(0) - 1)
    def _():
        factor = jnp.exp2(2.0 * LOG2E * (AMP - GAMMA * row_squares(points_ref[...])))
        fit_ref[...] = sum_ref[...] * (factor * (1.0 / math.sqrt(CENTERS)))


def fit_call(points, centers, direction, cols=2048, tile_rows=256):
    rows, count = points.shape[0], centers.shape[0]
    return pl.pallas_call(
        functools.partial(fit_kernel, tile_rows),
        grid=(count // cols,),
        in_specs=[
            pl.BlockSpec((rows, WIDTH), lambda j: (0, 0)),
            pl.BlockSpec((cols, WIDTH), lambda j: (j, 0)),
            pl.BlockSpec((cols, WIDTH), lambda j: (j, 0)),
        ],
        out_specs=[VMEM, VMEM],
        out_shape=[pltpu.VMEM((rows, count), BF16), pltpu.VMEM((rows, WIDTH), F32)],
        scratch_shapes=[
            pltpu.VMEM((rows, 2 * WIDTH), BF16),
            pltpu.VMEM((2 * WIDTH, cols), BF16),
            pltpu.VMEM((cols, WIDTH), BF16),
            pltpu.VMEM((rows, WIDTH), F32),
        ],
        compiler_params=pltpu.CompilerParams(vmem_limit_bytes=30 * 2**20),
        name="fit_tiles",
    )(points, centers, direction)


def back_kernel(other, first, fitted_ref, tile_ref, out_ref, turned_ref):
    step = pl.program_id(0)
    cols = out_ref.shape[0] // pl.num_programs(0)

    @pl.when(step == 0)
    def _():
        turned = fitted_ref[...].astype(F32).T * (1.0 / math.sqrt(POINTS))
        turned_ref[...] = turned.astype(BF16)

    piece = owner(lax.axis_index("dp"), first + step, other)
    tile = tile_ref[:, pl.ds(pl.multiple_of(piece * cols, cols), cols)]
    out = jnp.dot(turned_ref[...], tile, preferred_element_type=F32).T
    out_ref[pl.ds(pl.multiple_of(step * cols, cols), cols), :] = out.astype(BF16)


def back_call(fitted, tiles, other, first, number):
    rows, count = tiles.shape
    return pl.pallas_call(
        functools.partial(back_kernel, other, first),
        grid=(number,),
        in_specs=[VMEM, VMEM],
        out_specs=VMEM,
        out_shape=pltpu.VMEM((number * count // 8, WIDTH), BF16),
        scratch_shapes=[pltpu.VMEM((WIDTH, rows), BF16)],
        compiler_params=pltpu.CompilerParams(vmem_limit_bytes=30 * 2**20),
        name="back_tiles",
    )(on_chip(fitted), on_chip(tiles))


def sum_kernel(in_ref, out_ref):
    total = in_ref[0].astype(F32)
    for k in range(1, in_ref.shape[0]):
        total += in_ref[k].astype(F32)
    total = total.astype(BF16)
    for k in range(in_ref.shape[0]):
        out_ref[k] = total


def sum_call(pieces):
    return pl.pallas_call(
        sum_kernel,
        in_specs=[VMEM],
        out_specs=VMEM,
        out_shape=pltpu.VMEM(pieces.shape, BF16),
        compiler_params=pltpu.CompilerParams(vmem_limit_bytes=4 * 2**20),
        name="sum_pieces",
    )(on_chip(pieces))


def add_kernel(a_ref, b_ref, *out_refs):
    size = out_refs[0].shape[0]
    for k, out_ref in enumerate(out_refs):
        at = slice(k * size, (k + 1) * size)
        out_ref[...] = (a_ref[at, :].astype(F32) + b_ref[at, :].astype(F32)).astype(BF16)


def add_call(a, b, number):
    return pl.pallas_call(
        add_kernel,
        in_specs=[VMEM, VMEM],
        out_specs=[VMEM] * number,
        out_shape=[pltpu.VMEM((a.shape[0] // number, WIDTH), BF16)] * number,
        compiler_params=pltpu.CompilerParams(vmem_limit_bytes=4 * 2**20),
        name="add_cores",
    )(on_chip(a), on_chip(b))


def gather_kernel(own_ref, first_ref, *refs):
    *more, out_ref = refs
    core = lax.axis_index("dp") & 1
    total = jnp.where(core == 0, own_ref[...].astype(F32), first_ref[...].astype(F32))
    for ref in more:
        total += ref[...].astype(F32)
    out_ref[...] = total


def gather_call(own, pieces):
    return pl.pallas_call(
        gather_kernel,
        in_specs=[VMEM] * (1 + len(pieces)),
        out_specs=VMEM,
        out_shape=pltpu.VMEM(own.shape, F32),
        compiler_params=pltpu.CompilerParams(vmem_limit_bytes=4 * 2**20),
        name="sum_chips",
    )(on_chip(own), *[on_chip(p) for p in pieces])


def widen_kernel(other, first, picks, *refs):
    *parts, out_ref, wide_ref, sems = refs
    me = lax.axis_index("dp")
    core = (me & 1) ^ other
    block = parts[0].shape[0]
    copies = []
    for j, choice in enumerate(picks):
        if choice[0] == choice[1]:
            wide_ref[j] = parts[choice[0]][...].astype(F32)
        else:
            zero = parts[choice[0]][...].astype(F32)
            one = parts[choice[1]][...].astype(F32)
            wide_ref[j] = jnp.where(core == 0, zero, one)
        at = pl.ds(pl.multiple_of(owner(me, first + j, other) * block, block), block)
        copies.append(pltpu.make_async_copy(wide_ref.at[j], out_ref.at[at, :], sems.at[j]))
        copies[-1].start()
    for copy in copies:
        copy.wait()


def widen_call(parts, other, first, picks, base=None):
    block = parts[0].shape[0]
    more = [] if base is None else [base]
    count = len(parts)

    def kernel(*refs):
        widen_kernel(other, first, picks, *refs[:count], *refs[count + len(more) :])

    hbm = pl.BlockSpec(memory_space=pl.ANY)
    return pl.pallas_call(
        kernel,
        in_specs=[VMEM] * count + [hbm] * len(more),
        out_specs=hbm,
        out_shape=jax.ShapeDtypeStruct((8 * block, WIDTH), F32),
        input_output_aliases={count: 0} if more else {},
        scratch_shapes=[pltpu.VMEM((len(picks), block, WIDTH), F32), pltpu.SemaphoreType.DMA((len(picks),))],
        compiler_params=pltpu.CompilerParams(vmem_limit_bytes=4 * 2**20),
        name="widen",
    )(*[on_chip(p) for p in parts], *more)


def per_device(points, centers, direction):
    rows, count = points.shape[0], centers.shape[0]
    groups = lax.axis_size("center")
    swap = [(i, i ^ 1) for i in range(16)]

    tiles, partial_fit = fit_call(in_hbm(points), in_hbm(centers), in_hbm(direction))
    part = rows // groups
    pieces = lax.all_to_all(partial_fit.reshape(groups, part, WIDTH), "center", 0, 0)
    fitted = lax.all_to_all(sum_call(pieces), "center", 0, 0).reshape(rows, WIDTH)

    received = lax.ppermute(back_call(fitted, tiles, 1, 0, SETS), "dp", swap)
    sends = add_call(back_call(fitted, tiles, 0, 0, SETS), received, SETS)
    pieces = [exchange(sends[j], j) for j in range(SETS)]
    partial = gather_call(sends[0], pieces)
    (full,) = add_call(partial, lax.ppermute(partial, "dp", swap), 1)
    pieces = [exchange(full, j) for j in range(SETS)]
    others = [lax.ppermute(p, "dp", swap) for p in pieces]
    out = widen_call([full] + pieces, 0, 0, [(0, 1), (2, 2), (3, 3), (4, 4)])
    return widen_call([full] + others, 1, 0, [(0, 1), (2, 2), (3, 3), (4, 4)], out)


def solution(mesh):
    return jax.shard_map(
        per_device,
        mesh=mesh,
        in_specs=(P("dp", None), P("center", None), P("center", None)),
        out_specs=P("center", None),
        check_vma=False,
    )
```

```python
import functools
import math

import jax
import jax.numpy as jnp
from jax import lax
from jax.experimental import pallas as pl
from jax.experimental.pallas import tpu as pltpu
from jax.sharding import PartitionSpec as P

CENTERS = 65536
POINTS = 24576
WIDTH = 128
GAMMA = 6.4 / WIDTH
AMP = 0.5 * WIDTH * math.log1p(4.0 * GAMMA)
LOG2E = math.log2(math.e)
CROSS_SCALE = 2.0 * GAMMA * LOG2E
BF16 = jnp.bfloat16
F32 = jnp.float32
ROWS_BY_ROWS = (((1,), (1,)), ((), ()))


def split_bf16(x):
    high = x.astype(BF16)
    return high, (x - high.astype(F32)).astype(BF16)


def row_squares(x):
    x = x.astype(F32)
    return jnp.sum(x * x, axis=1, keepdims=True)


VMEM = pl.BlockSpec(memory_space=pltpu.VMEM)

OFFSETS = ((4, 6, 1, 0), (5, 3, 7, 2))
RELAY = (2, 6)
SETS = len(OFFSETS[0])
PACKED = [sum(k << (4 * j) for j, k in enumerate(row)) for row in OFFSETS]


def owner(me, j, other):
    table = jnp.where((me & 1) == other, PACKED[0], PACKED[1])
    return (me >> 1) ^ ((table >> (4 * j)) & 7)


def exchange(x, hops):
    pairs = [(2 * chip + c, 2 * (chip ^ hops[c]) + c) for chip in range(8) for c in range(2) if hops[c]]
    return lax.ppermute(x, "dp", pairs)


def on_chip(x):
    return pltpu.with_memory_space_constraint(x, pltpu.VMEM)


def in_hbm(x):
    return pltpu.with_memory_space_constraint(x, pltpu.HBM)


def fit_kernel(tile_rows, points_ref, centers_ref, direction_ref, tile_ref, fit_ref, scaled_ref, turned_ref, weights_ref, sum_ref):
    step = pl.program_id(0)
    rows = points_ref.shape[0]
    cols = centers_ref.shape[0]

    @pl.when(step == 0)
    def _():
        high, low = split_bf16(points_ref[...].astype(F32) * CROSS_SCALE)
        scaled_ref[:, :WIDTH] = high
        scaled_ref[:, WIDTH:] = low
        sum_ref[...] = jnp.zeros_like(sum_ref)

    turned = centers_ref[...].astype(F32).T
    shift = jnp.sum(turned * turned, axis=0, keepdims=True) * (-GAMMA * LOG2E)
    turned = turned.astype(BF16)
    turned_ref[:WIDTH, :] = turned
    turned_ref[WIDTH:, :] = turned
    weights_ref[...] = direction_ref[...].astype(BF16)

    def make(t):
        at = slice(t * tile_rows, (t + 1) * tile_rows)
        cross = jnp.dot(scaled_ref[at, :], turned_ref[...], preferred_element_type=F32)
        tile = jnp.exp2(cross + shift).astype(BF16)
        tile_ref[at, pl.ds(pl.multiple_of(step * cols, cols), cols)] = tile
        return tile

    def fit(t, tile):
        at = slice(t * tile_rows, (t + 1) * tile_rows)
        sum_ref[at, :] += jnp.dot(tile, weights_ref[...], preferred_element_type=F32)

    count = rows // tile_rows
    last = make(0)
    for t in range(1, count):
        tile = make(t)
        fit(t - 1, last)
        last = tile
    fit(count - 1, last)

    @pl.when(step == pl.num_programs(0) - 1)
    def _():
        factor = jnp.exp2(2.0 * LOG2E * (AMP - GAMMA * row_squares(points_ref[...])))
        fit_ref[...] = sum_ref[...] * (factor * (1.0 / math.sqrt(CENTERS)))


def fit_call(points, centers, direction, cols=2048, tile_rows=256):
    rows, count = points.shape[0], centers.shape[0]
    return pl.pallas_call(
        functools.partial(fit_kernel, tile_rows),
        grid=(count // cols,),
        in_specs=[
            pl.BlockSpec((rows, WIDTH), lambda j: (0, 0)),
            pl.BlockSpec((cols, WIDTH), lambda j: (j, 0)),
            pl.BlockSpec((cols, WIDTH), lambda j: (j, 0)),
        ],
        out_specs=[VMEM, VMEM],
        out_shape=[pltpu.VMEM((rows, count), BF16), pltpu.VMEM((rows, WIDTH), F32)],
        scratch_shapes=[
            pltpu.VMEM((rows, 2 * WIDTH), BF16),
            pltpu.VMEM((2 * WIDTH, cols), BF16),
            pltpu.VMEM((cols, WIDTH), BF16),
            pltpu.VMEM((rows, WIDTH), F32),
        ],
        compiler_params=pltpu.CompilerParams(vmem_limit_bytes=30 * 2**20),
        name="fit_tiles",
    )(points, centers, direction)


def back_kernel(other, picks, fitted_ref, tile_ref, out_ref):
    size = out_ref.shape[0] // len(picks)
    me = lax.axis_index("dp")
    turned = fitted_ref[...].astype(F32).T * (1.0 / math.sqrt(POINTS))
    turned = turned.astype(BF16)
    for n, j in enumerate(picks):
        first = owner(me, j, other) * size
        tile = tile_ref[:, pl.ds(pl.multiple_of(first, size), size)]
        out = jnp.dot(turned, tile, preferred_element_type=F32).T
        out_ref[n * size : (n + 1) * size, :] = out.astype(BF16)


def back_call(fitted, tiles, other, picks):
    rows, count = tiles.shape
    return pl.pallas_call(
        functools.partial(back_kernel, other, picks),
        in_specs=[VMEM, VMEM],
        out_specs=VMEM,
        out_shape=pltpu.VMEM((len(picks) * count // 8, WIDTH), BF16),
        compiler_params=pltpu.CompilerParams(vmem_limit_bytes=30 * 2**20),
        name="back_tiles",
    )(on_chip(fitted), on_chip(tiles))


def sum_kernel(in_ref, out_ref):
    total = in_ref[0].astype(F32)
    for k in range(1, in_ref.shape[0]):
        total += in_ref[k].astype(F32)
    total = total.astype(BF16)
    for k in range(in_ref.shape[0]):
        out_ref[k] = total


def sum_call(pieces):
    return pl.pallas_call(
        sum_kernel,
        in_specs=[VMEM],
        out_specs=VMEM,
        out_shape=pltpu.VMEM(pieces.shape, BF16),
        compiler_params=pltpu.CompilerParams(vmem_limit_bytes=4 * 2**20),
        name="sum_pieces",
    )(on_chip(pieces))


def add_kernel(a_ref, b_ref, *out_refs):
    size = out_refs[0].shape[0]
    for k, out_ref in enumerate(out_refs):
        at = slice(k * size, (k + 1) * size)
        out_ref[...] = (a_ref[at, :].astype(F32) + b_ref[at, :].astype(F32)).astype(BF16)


def add_call(a, b, number):
    return pl.pallas_call(
        add_kernel,
        in_specs=[VMEM, VMEM],
        out_specs=[VMEM] * number,
        out_shape=[pltpu.VMEM((a.shape[0] // number, WIDTH), BF16)] * number,
        compiler_params=pltpu.CompilerParams(vmem_limit_bytes=4 * 2**20),
        name="add_cores",
    )(on_chip(a), on_chip(b))


def gather_kernel(own_ref, first_ref, *refs):
    *more, out_ref = refs
    core = lax.axis_index("dp") & 1
    total = jnp.where(core == 0, own_ref[...].astype(F32), first_ref[...].astype(F32))
    for ref in more:
        total += ref[...].astype(F32)
    out_ref[...] = total


def gather_call(own, pieces):
    return pl.pallas_call(
        gather_kernel,
        in_specs=[VMEM] * (1 + len(pieces)),
        out_specs=VMEM,
        out_shape=pltpu.VMEM(own.shape, F32),
        compiler_params=pltpu.CompilerParams(vmem_limit_bytes=4 * 2**20),
        name="sum_chips",
    )(on_chip(own), *[on_chip(p) for p in pieces])


def widen_kernel(picks, *refs):
    *parts, out_ref, wide_ref, sems = refs
    me = lax.axis_index("dp")
    block = parts[0].shape[0]
    copies = []
    for n, (other, j, choice) in enumerate(picks):
        if choice[0] == choice[1]:
            wide_ref[n] = parts[choice[0]][...].astype(F32)
        else:
            zero = parts[choice[0]][...].astype(F32)
            one = parts[choice[1]][...].astype(F32)
            wide_ref[n] = jnp.where((me & 1) == other, zero, one)
        at = pl.ds(pl.multiple_of(owner(me, j, other) * block, block), block)
        copies.append(pltpu.make_async_copy(wide_ref.at[n], out_ref.at[at, :], sems.at[n]))
        copies[-1].start()
    for copy in copies:
        copy.wait()


def widen_call(parts, picks, base=None):
    block = parts[0].shape[0]
    more = [] if base is None else [base]
    count = len(parts)

    def kernel(*refs):
        widen_kernel(picks, *refs[:count], *refs[count + len(more) :])

    hbm = pl.BlockSpec(memory_space=pl.ANY)
    return pl.pallas_call(
        kernel,
        in_specs=[VMEM] * count + [hbm] * len(more),
        out_specs=hbm,
        out_shape=jax.ShapeDtypeStruct((8 * block, WIDTH), F32),
        input_output_aliases={count: 0} if more else {},
        scratch_shapes=[pltpu.VMEM((len(picks), block, WIDTH), F32), pltpu.SemaphoreType.DMA((len(picks),))],
        compiler_params=pltpu.CompilerParams(vmem_limit_bytes=4 * 2**20),
        name="widen",
    )(*[on_chip(p) for p in parts], *more)


def per_device(points, centers, direction):
    rows, count = points.shape[0], centers.shape[0]
    groups = lax.axis_size("center")
    swap = [(i, i ^ 1) for i in range(16)]

    tiles, partial_fit = fit_call(in_hbm(points), in_hbm(centers), in_hbm(direction))
    part = rows // groups
    pieces = lax.all_to_all(partial_fit.reshape(groups, part, WIDTH), "center", 0, 0)
    fitted = lax.all_to_all(sum_call(pieces), "center", 0, 0).reshape(rows, WIDTH)

    sends = {}
    halves = ((0, 2), (1, 3))
    received = [lax.ppermute(back_call(fitted, tiles, 1, picks), "dp", swap) for picks in halves]
    for picks, r in zip(halves, received):
        sends.update(zip(picks, add_call(back_call(fitted, tiles, 0, picks), r, len(picks))))
    hops = [tuple(row[j] for row in OFFSETS) for j in range(SETS)]
    (relayed,) = add_call(sends[1], exchange(sends[0], RELAY), 1)
    pieces = [exchange(x, h) for x, h in zip((sends[3], sends[2], relayed), hops[:0:-1])]
    partial = gather_call(sends[3], pieces)
    (full,) = add_call(partial, lax.ppermute(partial, "dp", swap), 1)
    pieces = [exchange(full, h) for h in hops[1:]]
    pieces = [exchange(pieces[0], RELAY)] + pieces
    others = [None] + [lax.ppermute(p, "dp", swap) for p in pieces[1:]]

    def write(out, *picks):
        parts, chosen = [full], []
        for other, j in picks:
            parts.append((others if other else pieces)[j])
            chosen.append((other, j, (0 if j == 3 else len(parts) - 1, len(parts) - 1)))
        return widen_call(parts, chosen, out)

    out = write(None, (0, 1), (0, 2), (0, 3), (1, 1))
    pieces[0], out = lax.optimization_barrier((pieces[0], out))
    others[0] = lax.ppermute(pieces[0], "dp", swap)
    out = write(out, (1, 2), (1, 3), (0, 0))
    return write(out, (1, 0))


def solution(mesh):
    return jax.shard_map(
        per_device,
        mesh=mesh,
        in_specs=(P("dp", None), P("center", None), P("center", None)),
        out_specs=P("center", None),
        check_vma=False,
    )
```

```python
import functools
import math

import jax
import jax.numpy as jnp
from jax import lax
from jax.experimental import pallas as pl
from jax.experimental.pallas import tpu as pltpu
from jax.sharding import PartitionSpec as P

CENTERS = 65536
POINTS = 24576
WIDTH = 128
GAMMA = 6.4 / WIDTH
AMP = 0.5 * WIDTH * math.log1p(4.0 * GAMMA)
LOG2E = math.log2(math.e)
CROSS_SCALE = 2.0 * GAMMA * LOG2E
BF16 = jnp.bfloat16
F32 = jnp.float32
ROWS_BY_ROWS = (((1,), (1,)), ((), ()))


def split_bf16(x):
    high = x.astype(BF16)
    return high, (x - high.astype(F32)).astype(BF16)


def row_squares(x):
    x = x.astype(F32)
    return jnp.sum(x * x, axis=1, keepdims=True)


VMEM = pl.BlockSpec(memory_space=pltpu.VMEM)

OFFSETS = ((4, 6, 1, 0), (5, 3, 7, 2))
RELAY = (2, 6)
SETS = len(OFFSETS[0])
PACKED = [sum(k << (4 * j) for j, k in enumerate(row)) for row in OFFSETS]


def owner(me, j, other):
    table = jnp.where((me & 1) == other, PACKED[0], PACKED[1])
    return (me >> 1) ^ ((table >> (4 * j)) & 7)


def exchange(x, hops):
    pairs = [(2 * chip + c, 2 * (chip ^ hops[c]) + c) for chip in range(8) for c in range(2) if hops[c]]
    return lax.ppermute(x, "dp", pairs)


def on_chip(x):
    return pltpu.with_memory_space_constraint(x, pltpu.VMEM)


def in_hbm(x):
    return pltpu.with_memory_space_constraint(x, pltpu.HBM)


def fit_kernel(tile_rows, points_ref, centers_ref, direction_ref, tile_ref, fit_ref, scaled_ref, turned_ref, weights_ref, sum_ref):
    step = pl.program_id(0)
    rows = points_ref.shape[0]
    cols = centers_ref.shape[0]

    @pl.when(step == 0)
    def _():
        high, low = split_bf16(points_ref[...].astype(F32) * CROSS_SCALE)
        scaled_ref[:, :WIDTH] = high
        scaled_ref[:, WIDTH:] = low
        sum_ref[...] = jnp.zeros_like(sum_ref)

    turned = centers_ref[...].astype(F32).T
    shift = jnp.sum(turned * turned, axis=0, keepdims=True) * (-GAMMA * LOG2E)
    turned = turned.astype(BF16)
    turned_ref[:WIDTH, :] = turned
    turned_ref[WIDTH:, :] = turned
    weights_ref[...] = direction_ref[...].astype(BF16)

    def make(t):
        at = slice(t * tile_rows, (t + 1) * tile_rows)
        cross = jnp.dot(scaled_ref[at, :], turned_ref[...], preferred_element_type=F32)
        tile = jnp.exp2(cross + shift).astype(BF16)
        tile_ref[at, pl.ds(pl.multiple_of(step * cols, cols), cols)] = tile
        return tile

    def fit(t, tile):
        at = slice(t * tile_rows, (t + 1) * tile_rows)
        sum_ref[at, :] += jnp.dot(tile, weights_ref[...], preferred_element_type=F32)

    count = rows // tile_rows
    made = []
    for t in range(count + 2):
        if t < count:
            made.append(make(t))
        if t >= 2:
            fit(t - 2, made[t - 2])

    @pl.when(step == pl.num_programs(0) - 1)
    def _():
        factor = jnp.exp2(2.0 * LOG2E * (AMP - GAMMA * row_squares(points_ref[...])))
        fit_ref[...] = sum_ref[...] * (factor * (1.0 / math.sqrt(CENTERS)))


def fit_call(points, centers, direction, cols=2048, tile_rows=256):
    rows, count = points.shape[0], centers.shape[0]
    return pl.pallas_call(
        functools.partial(fit_kernel, tile_rows),
        grid=(count // cols,),
        in_specs=[
            pl.BlockSpec((rows, WIDTH), lambda j: (0, 0)),
            pl.BlockSpec((cols, WIDTH), lambda j: (j, 0)),
            pl.BlockSpec((cols, WIDTH), lambda j: (j, 0)),
        ],
        out_specs=[VMEM, VMEM],
        out_shape=[pltpu.VMEM((rows, count), BF16), pltpu.VMEM((rows, WIDTH), F32)],
        scratch_shapes=[
            pltpu.VMEM((rows, 2 * WIDTH), BF16),
            pltpu.VMEM((2 * WIDTH, cols), BF16),
            pltpu.VMEM((cols, WIDTH), BF16),
            pltpu.VMEM((rows, WIDTH), F32),
        ],
        compiler_params=pltpu.CompilerParams(vmem_limit_bytes=30 * 2**20),
        name="fit_tiles",
    )(points, centers, direction)


def back_kernel(other, picks, fitted_ref, tile_ref, *refs):
    *received, first_ref = refs[: len(refs) - (1 if other else len(picks)) + 1]
    out_refs = refs[len(received) :]
    size = first_ref.shape[0] // (len(picks) if other else 1)
    me = lax.axis_index("dp")
    turned = fitted_ref[...].astype(F32).T * (1.0 / math.sqrt(POINTS))
    turned = turned.astype(BF16)
    for n, j in enumerate(picks):
        first = owner(me, j, other) * size
        tile = tile_ref[:, pl.ds(pl.multiple_of(first, size), size)]
        out = jnp.dot(turned, tile, preferred_element_type=F32).T
        at = slice(n * size, (n + 1) * size)
        if other:
            first_ref[at, :] = out.astype(BF16)
        else:
            out_refs[n][...] = (out + received[0][at, :].astype(F32)).astype(BF16)


def back_call(fitted, tiles, other, picks, *received):
    rows, count = tiles.shape
    each = 1 if other else len(picks)
    return pl.pallas_call(
        functools.partial(back_kernel, other, picks),
        in_specs=[VMEM] * (2 + len(received)),
        out_specs=[VMEM] * each,
        out_shape=[pltpu.VMEM((len(picks) * count // 8 // each, WIDTH), BF16)] * each,
        compiler_params=pltpu.CompilerParams(vmem_limit_bytes=30 * 2**20),
        name="back_tiles",
    )(on_chip(fitted), on_chip(tiles), *[on_chip(r) for r in received])


def sum_kernel(in_ref, out_ref):
    total = in_ref[0].astype(F32)
    for k in range(1, in_ref.shape[0]):
        total += in_ref[k].astype(F32)
    total = total.astype(BF16)
    for k in range(in_ref.shape[0]):
        out_ref[k] = total


def sum_call(pieces):
    return pl.pallas_call(
        sum_kernel,
        in_specs=[VMEM],
        out_specs=VMEM,
        out_shape=pltpu.VMEM(pieces.shape, BF16),
        compiler_params=pltpu.CompilerParams(vmem_limit_bytes=4 * 2**20),
        name="sum_pieces",
    )(on_chip(pieces))


def add_kernel(a_ref, b_ref, out_ref):
    out_ref[...] = (a_ref[...].astype(F32) + b_ref[...].astype(F32)).astype(BF16)


def add_call(a, b):
    return pl.pallas_call(
        add_kernel,
        in_specs=[VMEM, VMEM],
        out_specs=VMEM,
        out_shape=pltpu.VMEM(a.shape, BF16),
        compiler_params=pltpu.CompilerParams(vmem_limit_bytes=4 * 2**20),
        name="add_pieces",
    )(on_chip(a), on_chip(b))


def begin_kernel(own_ref, along_ref, out_ref):
    own = jnp.where((lax.axis_index("dp") & 1) == 0, own_ref[...].astype(F32), 0.0)
    out_ref[...] = own + along_ref[...].astype(F32)


def finish_kernel(begun_ref, aside_ref, relayed_ref, out_ref):
    out_ref[...] = begun_ref[...] + aside_ref[...].astype(F32) + relayed_ref[...].astype(F32)


def gather_call(kernel, *pieces):
    return pl.pallas_call(
        kernel,
        in_specs=[VMEM] * len(pieces),
        out_specs=VMEM,
        out_shape=pltpu.VMEM(pieces[0].shape, F32),
        compiler_params=pltpu.CompilerParams(vmem_limit_bytes=4 * 2**20),
        name="sum_chips",
    )(*[on_chip(p) for p in pieces])


def widen_kernel(picks, *refs):
    *parts, out_ref, wide_ref, sems = refs
    me = lax.axis_index("dp")
    block = parts[0].shape[0]
    copies = []
    for n, (other, j, choice) in enumerate(picks):
        if choice[0] == choice[1]:
            wide_ref[n] = parts[choice[0]][...].astype(F32)
        else:
            zero = parts[choice[0]][...].astype(F32)
            one = parts[choice[1]][...].astype(F32)
            wide_ref[n] = jnp.where((me & 1) == other, zero, one)
        at = pl.ds(pl.multiple_of(owner(me, j, other) * block, block), block)
        copies.append(pltpu.make_async_copy(wide_ref.at[n], out_ref.at[at, :], sems.at[n]))
        copies[-1].start()
    for copy in copies:
        copy.wait()


def widen_call(parts, picks, base=None):
    block = parts[0].shape[0]
    more = [] if base is None else [base]
    count = len(parts)

    def kernel(*refs):
        widen_kernel(picks, *refs[:count], *refs[count + len(more) :])

    hbm = pl.BlockSpec(memory_space=pl.ANY)
    return pl.pallas_call(
        kernel,
        in_specs=[VMEM] * count + [hbm] * len(more),
        out_specs=hbm,
        out_shape=jax.ShapeDtypeStruct((8 * block, WIDTH), F32),
        input_output_aliases={count: 0} if more else {},
        scratch_shapes=[pltpu.VMEM((len(picks), block, WIDTH), F32), pltpu.SemaphoreType.DMA((len(picks),))],
        compiler_params=pltpu.CompilerParams(vmem_limit_bytes=4 * 2**20),
        name="widen",
    )(*[on_chip(p) for p in parts], *more)


def per_device(points, centers, direction):
    rows, count = points.shape[0], centers.shape[0]
    groups = lax.axis_size("center")
    swap = [(i, i ^ 1) for i in range(16)]

    tiles, partial_fit = fit_call(in_hbm(points), in_hbm(centers), in_hbm(direction))
    part = rows // groups
    pieces = lax.all_to_all(partial_fit.reshape(groups, part, WIDTH), "center", 0, 0)
    fitted = lax.all_to_all(sum_call(pieces), "center", 0, 0).reshape(rows, WIDTH)

    sends = {}
    halves = ((0, 2), (1, 3))
    received = [lax.ppermute(back_call(fitted, tiles, 1, picks)[0], "dp", swap) for picks in halves]
    for picks, r in zip(halves, received):
        sends.update(zip(picks, back_call(fitted, tiles, 0, picks, r)))
    hops = [tuple(row[j] for row in OFFSETS) for j in range(SETS)]
    relay = exchange(sends[0], RELAY)
    along = exchange(sends[2], hops[2])
    aside = exchange(sends[3], hops[3])
    relayed = add_call(sends[1], relay)
    begun = gather_call(begin_kernel, sends[3], along)
    partial = gather_call(finish_kernel, begun, aside, exchange(relayed, hops[1]))
    full = add_call(partial, lax.ppermute(partial, "dp", swap))
    pieces = [exchange(full, h) for h in hops[1:]]
    pieces = [exchange(pieces[0], RELAY)] + pieces
    others = [None] + [lax.ppermute(p, "dp", swap) for p in pieces[1:]]

    def write(out, *picks):
        parts, chosen = [full], []
        for other, j in picks:
            parts.append((others if other else pieces)[j])
            chosen.append((other, j, (0 if j == 3 else len(parts) - 1, len(parts) - 1)))
        return widen_call(parts, chosen, out)

    out = write(None, (0, 1), (0, 2), (0, 3), (1, 1))
    pieces[0], out = lax.optimization_barrier((pieces[0], out))
    others[0] = lax.ppermute(pieces[0], "dp", swap)
    out = write(out, (1, 2), (1, 3), (0, 0))
    return write(out, (1, 0))


def solution(mesh):
    return jax.shard_map(
        per_device,
        mesh=mesh,
        in_specs=(P("dp", None), P("center", None), P("center", None)),
        out_specs=P("center", None),
        check_vma=False,
    )
```

```python
import functools
import math

import jax
import jax.numpy as jnp
from jax import lax
from jax.experimental import pallas as pl
from jax.experimental.pallas import tpu as pltpu
from jax.sharding import PartitionSpec as P

CENTERS = 65536
POINTS = 24576
WIDTH = 128
GAMMA = 6.4 / WIDTH
AMP = 0.5 * WIDTH * math.log1p(4.0 * GAMMA)
LOG2E = math.log2(math.e)
CROSS_SCALE = 2.0 * GAMMA * LOG2E
BF16 = jnp.bfloat16
F32 = jnp.float32
ROWS_BY_ROWS = (((1,), (1,)), ((), ()))


def split_bf16(x):
    high = x.astype(BF16)
    return high, (x - high.astype(F32)).astype(BF16)


def row_squares(x):
    x = x.astype(F32)
    return jnp.sum(x * x, axis=1, keepdims=True)


VMEM = pl.BlockSpec(memory_space=pltpu.VMEM)

OFFSETS = ((4, 6, 1, 0), (5, 3, 7, 2))
RELAY = (2, 6)
SETS = len(OFFSETS[0])
PACKED = [sum(k << (4 * j) for j, k in enumerate(row)) for row in OFFSETS]


def owner(me, j, other):
    table = jnp.where((me & 1) == other, PACKED[0], PACKED[1])
    return (me >> 1) ^ ((table >> (4 * j)) & 7)


def exchange(x, hops):
    pairs = [(2 * chip + c, 2 * (chip ^ hops[c]) + c) for chip in range(8) for c in range(2) if hops[c]]
    return lax.ppermute(x, "dp", pairs)


def on_chip(x):
    return pltpu.with_memory_space_constraint(x, pltpu.VMEM)


def in_hbm(x):
    return pltpu.with_memory_space_constraint(x, pltpu.HBM)


def fit_kernel(cols, tile_rows, lag, points_hbm, centers_hbm, direction_hbm, tile_ref, fit_ref, *scratch):
    points_ref, centers_ref, direction_ref, scaled_ref, turned_ref, weights_ref, sum_ref, sems = scratch
    rows, count = points_ref.shape[0], centers_ref.shape[0]
    blocks = count // cols

    def block(b):
        return slice(b * cols, (b + 1) * cols)

    load_points = pltpu.make_async_copy(points_hbm, points_ref, sems.at[2 * blocks])
    load_points.start()
    loads = []
    for b in range(blocks):
        pairs = ((centers_hbm, centers_ref), (direction_hbm, direction_ref))
        for k, (source, target) in enumerate(pairs):
            loads.append(pltpu.make_async_copy(source.at[block(b), :], target.at[block(b), :], sems.at[2 * b + k]))
            loads[-1].start()

    load_points.wait()
    high, low = split_bf16(points_ref[...].astype(F32) * CROSS_SCALE)
    scaled_ref[:, :WIDTH] = high
    scaled_ref[:, WIDTH:] = low

    def prepare(b):
        loads[2 * b].wait()
        turned = centers_ref[block(b), :].astype(F32).T
        shift = jnp.sum(turned * turned, axis=0, keepdims=True) * (-GAMMA * LOG2E)
        turned = turned.astype(BF16)
        turned_ref[:WIDTH, block(b)] = turned
        turned_ref[WIDTH:, block(b)] = turned
        loads[2 * b + 1].wait()
        weights_ref[block(b), :] = direction_ref[block(b), :].astype(BF16)
        return shift

    def make(b, t, shift):
        at = slice(t * tile_rows, (t + 1) * tile_rows)
        cross = jnp.dot(scaled_ref[at, :], turned_ref[:, block(b)], preferred_element_type=F32)
        tile = jnp.exp2(cross + shift).astype(BF16)
        tile_ref[at, block(b)] = tile
        return tile

    def fit(b, t, tile):
        at = slice(t * tile_rows, (t + 1) * tile_rows)
        part = jnp.dot(tile, weights_ref[block(b), :], preferred_element_type=F32)
        if b == 0:
            sum_ref[at, :] = part
        else:
            sum_ref[at, :] += part

    steps = [(b, t) for b in range(blocks) for t in range(rows // tile_rows)]
    made = []
    shifts = [prepare(0)]
    for n in range(len(steps) + lag):
        if n < len(steps):
            b, t = steps[n]
            made.append(make(b, t, shifts[b]))
            if t == 2 and b + 1 < blocks:
                shifts.append(prepare(b + 1))
        if n >= lag:
            fit(*steps[n - lag], made[n - lag])

    factor = jnp.exp2(2.0 * LOG2E * (AMP - GAMMA * row_squares(points_ref[...])))
    fit_ref[...] = sum_ref[...] * (factor * (1.0 / math.sqrt(CENTERS)))


def fit_call(points, centers, direction, cols=4096, tile_rows=256, lag=1):
    rows, count = points.shape[0], centers.shape[0]
    hbm = pl.BlockSpec(memory_space=pl.ANY)
    return pl.pallas_call(
        functools.partial(fit_kernel, cols, tile_rows, lag),
        in_specs=[hbm] * 3,
        out_specs=[VMEM, VMEM],
        out_shape=[pltpu.VMEM((rows, count), BF16), pltpu.VMEM((rows, WIDTH), F32)],
        scratch_shapes=[
            pltpu.VMEM((rows, WIDTH), BF16),
            pltpu.VMEM((count, WIDTH), BF16),
            pltpu.VMEM((count, WIDTH), F32),
            pltpu.VMEM((rows, 2 * WIDTH), BF16),
            pltpu.VMEM((2 * WIDTH, count), BF16),
            pltpu.VMEM((count, WIDTH), BF16),
            pltpu.VMEM((rows, WIDTH), F32),
            pltpu.SemaphoreType.DMA((2 * (count // cols) + 1,)),
        ],
        compiler_params=pltpu.CompilerParams(vmem_limit_bytes=30 * 2**20),
        name="fit_tiles",
    )(points, centers, direction)


def back_kernel(other, picks, fitted_ref, tile_ref, *refs):
    *received, first_ref = refs[: len(refs) - (1 if other else len(picks)) + 1]
    out_refs = refs[len(received) :]
    size = first_ref.shape[0] // (len(picks) if other else 1)
    me = lax.axis_index("dp")
    turned = fitted_ref[...].astype(F32).T * (1.0 / math.sqrt(POINTS))
    turned = turned.astype(BF16)
    for n, j in enumerate(picks):
        first = owner(me, j, other) * size
        tile = tile_ref[:, pl.ds(pl.multiple_of(first, size), size)]
        out = jnp.dot(turned, tile, preferred_element_type=F32).T
        at = slice(n * size, (n + 1) * size)
        if other:
            first_ref[at, :] = out.astype(BF16)
        else:
            out_refs[n][...] = (out + received[0][at, :].astype(F32)).astype(BF16)


def back_call(fitted, tiles, other, picks, *received):
    rows, count = tiles.shape
    each = 1 if other else len(picks)
    return pl.pallas_call(
        functools.partial(back_kernel, other, picks),
        in_specs=[VMEM] * (2 + len(received)),
        out_specs=[VMEM] * each,
        out_shape=[pltpu.VMEM((len(picks) * count // 8 // each, WIDTH), BF16)] * each,
        compiler_params=pltpu.CompilerParams(vmem_limit_bytes=30 * 2**20),
        name="back_tiles",
    )(on_chip(fitted), on_chip(tiles), *[on_chip(r) for r in received])


def sum_kernel(in_ref, out_ref):
    total = in_ref[0].astype(F32)
    for k in range(1, in_ref.shape[0]):
        total += in_ref[k].astype(F32)
    total = total.astype(BF16)
    for k in range(in_ref.shape[0]):
        out_ref[k] = total


def sum_call(pieces):
    return pl.pallas_call(
        sum_kernel,
        in_specs=[VMEM],
        out_specs=VMEM,
        out_shape=pltpu.VMEM(pieces.shape, BF16),
        compiler_params=pltpu.CompilerParams(vmem_limit_bytes=4 * 2**20),
        name="sum_pieces",
    )(on_chip(pieces))


def add_kernel(a_ref, b_ref, out_ref):
    out_ref[...] = (a_ref[...].astype(F32) + b_ref[...].astype(F32)).astype(BF16)


def add_call(a, b):
    return pl.pallas_call(
        add_kernel,
        in_specs=[VMEM, VMEM],
        out_specs=VMEM,
        out_shape=pltpu.VMEM(a.shape, BF16),
        compiler_params=pltpu.CompilerParams(vmem_limit_bytes=4 * 2**20),
        name="add_pieces",
    )(on_chip(a), on_chip(b))


def begin_kernel(own_ref, along_ref, out_ref):
    own = jnp.where((lax.axis_index("dp") & 1) == 0, own_ref[...].astype(F32), 0.0)
    out_ref[...] = own + along_ref[...].astype(F32)


def finish_kernel(begun_ref, aside_ref, relayed_ref, out_ref):
    out_ref[...] = begun_ref[...] + aside_ref[...].astype(F32) + relayed_ref[...].astype(F32)


def gather_call(kernel, *pieces):
    return pl.pallas_call(
        kernel,
        in_specs=[VMEM] * len(pieces),
        out_specs=VMEM,
        out_shape=pltpu.VMEM(pieces[0].shape, F32),
        compiler_params=pltpu.CompilerParams(vmem_limit_bytes=4 * 2**20),
        name="sum_chips",
    )(*[on_chip(p) for p in pieces])


def widen_kernel(picks, *refs):
    *parts, out_ref, wide_ref, sems = refs
    me = lax.axis_index("dp")
    block = parts[0].shape[0]
    copies = []
    for n, (other, j, choice) in enumerate(picks):
        if choice[0] == choice[1]:
            wide_ref[n] = parts[choice[0]][...].astype(F32)
        else:
            zero = parts[choice[0]][...].astype(F32)
            one = parts[choice[1]][...].astype(F32)
            wide_ref[n] = jnp.where((me & 1) == other, zero, one)
        at = pl.ds(pl.multiple_of(owner(me, j, other) * block, block), block)
        copies.append(pltpu.make_async_copy(wide_ref.at[n], out_ref.at[at, :], sems.at[n]))
        copies[-1].start()
    for copy in copies:
        copy.wait()


def widen_call(parts, picks, base=None):
    block = parts[0].shape[0]
    more = [] if base is None else [base]
    count = len(parts)

    def kernel(*refs):
        widen_kernel(picks, *refs[:count], *refs[count + len(more) :])

    hbm = pl.BlockSpec(memory_space=pl.ANY)
    return pl.pallas_call(
        kernel,
        in_specs=[VMEM] * count + [hbm] * len(more),
        out_specs=hbm,
        out_shape=jax.ShapeDtypeStruct((8 * block, WIDTH), F32),
        input_output_aliases={count: 0} if more else {},
        scratch_shapes=[pltpu.VMEM((len(picks), block, WIDTH), F32), pltpu.SemaphoreType.DMA((len(picks),))],
        compiler_params=pltpu.CompilerParams(vmem_limit_bytes=4 * 2**20),
        name="widen",
    )(*[on_chip(p) for p in parts], *more)


def per_device(points, centers, direction):
    rows, count = points.shape[0], centers.shape[0]
    groups = lax.axis_size("center")
    swap = [(i, i ^ 1) for i in range(16)]

    tiles, partial_fit = fit_call(in_hbm(points), in_hbm(centers), in_hbm(direction))
    part = rows // groups
    pieces = lax.all_to_all(partial_fit.reshape(groups, part, WIDTH), "center", 0, 0)
    fitted = lax.all_to_all(sum_call(pieces), "center", 0, 0).reshape(rows, WIDTH)

    sends = {}
    halves = ((0, 2), (1, 3))
    received = [lax.ppermute(back_call(fitted, tiles, 1, picks)[0], "dp", swap) for picks in halves]
    for picks, r in zip(halves, received):
        sends.update(zip(picks, back_call(fitted, tiles, 0, picks, r)))
    hops = [tuple(row[j] for row in OFFSETS) for j in range(SETS)]
    relay = exchange(sends[0], RELAY)
    along = exchange(sends[2], hops[2])
    aside = exchange(sends[3], hops[3])
    relayed = add_call(sends[1], relay)
    begun = gather_call(begin_kernel, sends[3], along)
    partial = gather_call(finish_kernel, begun, aside, exchange(relayed, hops[1]))
    full = add_call(partial, lax.ppermute(partial, "dp", swap))
    pieces = [exchange(full, h) for h in hops[1:]]
    pieces = [exchange(pieces[0], RELAY)] + pieces
    others = [None] + [lax.ppermute(p, "dp", swap) for p in pieces[1:]]

    def write(out, *picks):
        parts, chosen = [full], []
        for other, j in picks:
            parts.append((others if other else pieces)[j])
            chosen.append((other, j, (0 if j == 3 else len(parts) - 1, len(parts) - 1)))
        return widen_call(parts, chosen, out)

    out = write(None, (0, 1), (0, 3), (1, 1))
    pieces[0], out = lax.optimization_barrier((pieces[0], out))
    others[0] = lax.ppermute(pieces[0], "dp", swap)
    out = write(out, (0, 2), (1, 3), (1, 2), (0, 0))
    return write(out, (1, 0))


def solution(mesh):
    return jax.shard_map(
        per_device,
        mesh=mesh,
        in_specs=(P("dp", None), P("center", None), P("center", None)),
        out_specs=P("center", None),
        check_vma=False,
    )
```

```python
import functools
import math

import jax
import jax.numpy as jnp
from jax import lax
from jax.experimental import pallas as pl
from jax.experimental.pallas import tpu as pltpu
from jax.sharding import PartitionSpec as P

CENTERS = 65536
POINTS = 24576
WIDTH = 128
GAMMA = 6.4 / WIDTH
AMP = 0.5 * WIDTH * math.log1p(4.0 * GAMMA)
LOG2E = math.log2(math.e)
CROSS_SCALE = 2.0 * GAMMA * LOG2E
BF16 = jnp.bfloat16
F32 = jnp.float32
ROWS_BY_ROWS = (((1,), (1,)), ((), ()))


def split_bf16(x):
    high = x.astype(BF16)
    return high, (x - high.astype(F32)).astype(BF16)


def row_squares(x):
    x = x.astype(F32)
    return jnp.sum(x * x, axis=1, keepdims=True)


VMEM = pl.BlockSpec(memory_space=pltpu.VMEM)

OFFSETS = ((4, 6, 1, 0), (5, 3, 7, 2))
RELAY = (2, 6)
SETS = len(OFFSETS[0])
PACKED = [sum(k << (4 * j) for j, k in enumerate(row)) for row in OFFSETS]


def owner(me, j, other):
    table = jnp.where((me & 1) == other, PACKED[0], PACKED[1])
    return (me >> 1) ^ ((table >> (4 * j)) & 7)


def exchange(x, hops):
    pairs = [(2 * chip + c, 2 * (chip ^ hops[c]) + c) for chip in range(8) for c in range(2) if hops[c]]
    return lax.ppermute(x, "dp", pairs)


def on_chip(x):
    return pltpu.with_memory_space_constraint(x, pltpu.VMEM)


def in_hbm(x):
    return pltpu.with_memory_space_constraint(x, pltpu.HBM)


def fit_kernel(cols, tile_rows, lag, points_hbm, centers_hbm, direction_hbm, tile_ref, fit_ref, *scratch):
    points_ref, centers_ref, direction_ref, scaled_ref, turned_ref, weights_ref, sum_ref, sems = scratch
    rows, count = points_ref.shape[0], centers_ref.shape[0]
    blocks = count // cols

    def block(b):
        return slice(b * cols, (b + 1) * cols)

    load_points = pltpu.make_async_copy(points_hbm, points_ref, sems.at[2 * blocks])
    load_points.start()
    loads = []
    for b in range(blocks):
        pairs = ((centers_hbm, centers_ref), (direction_hbm, direction_ref))
        for k, (source, target) in enumerate(pairs):
            loads.append(pltpu.make_async_copy(source.at[block(b), :], target.at[block(b), :], sems.at[2 * b + k]))
            loads[-1].start()

    load_points.wait()
    high, low = split_bf16(points_ref[...].astype(F32) * CROSS_SCALE)
    scaled_ref[:, :WIDTH] = high
    scaled_ref[:, WIDTH:] = low

    def prepare(b):
        loads[2 * b].wait()
        turned = centers_ref[block(b), :].astype(F32).T
        shift = jnp.sum(turned * turned, axis=0, keepdims=True) * (-GAMMA * LOG2E)
        turned = turned.astype(BF16)
        turned_ref[:WIDTH, block(b)] = turned
        turned_ref[WIDTH:, block(b)] = turned
        loads[2 * b + 1].wait()
        weights_ref[block(b), :] = direction_ref[block(b), :].astype(BF16)
        return shift

    def make(b, t, shift):
        at = slice(t * tile_rows, (t + 1) * tile_rows)
        cross = jnp.dot(scaled_ref[at, :], turned_ref[:, block(b)], preferred_element_type=F32)
        tile = jnp.exp2(cross + shift).astype(BF16)
        tile_ref[at, block(b)] = tile
        return tile

    def fit(b, t, tile):
        at = slice(t * tile_rows, (t + 1) * tile_rows)
        part = jnp.dot(tile, weights_ref[block(b), :], preferred_element_type=F32)
        if b == 0:
            sum_ref[at, :] = part
        else:
            sum_ref[at, :] += part

    steps = [(b, t) for b in range(blocks) for t in range(rows // tile_rows)]
    made = []
    shifts = [prepare(0)]
    for n in range(len(steps) + lag):
        if n < len(steps):
            b, t = steps[n]
            made.append(make(b, t, shifts[b]))
            if t == 2 and b + 1 < blocks:
                shifts.append(prepare(b + 1))
        if n >= lag:
            fit(*steps[n - lag], made[n - lag])

    factor = jnp.exp2(2.0 * LOG2E * (AMP - GAMMA * row_squares(points_ref[...])))
    fit_ref[...] = sum_ref[...] * (factor * (1.0 / math.sqrt(CENTERS)))


def fit_call(points, centers, direction, cols=4096, tile_rows=256, lag=1):
    rows, count = points.shape[0], centers.shape[0]
    hbm = pl.BlockSpec(memory_space=pl.ANY)
    return pl.pallas_call(
        functools.partial(fit_kernel, cols, tile_rows, lag),
        in_specs=[hbm] * 3,
        out_specs=[VMEM, VMEM],
        out_shape=[pltpu.VMEM((rows, count), BF16), pltpu.VMEM((rows, WIDTH), F32)],
        scratch_shapes=[
            pltpu.VMEM((rows, WIDTH), BF16),
            pltpu.VMEM((count, WIDTH), BF16),
            pltpu.VMEM((count, WIDTH), F32),
            pltpu.VMEM((rows, 2 * WIDTH), BF16),
            pltpu.VMEM((2 * WIDTH, count), BF16),
            pltpu.VMEM((count, WIDTH), BF16),
            pltpu.VMEM((rows, WIDTH), F32),
            pltpu.SemaphoreType.DMA((2 * (count // cols) + 1,)),
        ],
        compiler_params=pltpu.CompilerParams(vmem_limit_bytes=30 * 2**20),
        name="fit_tiles",
    )(points, centers, direction)


def back_kernel(other, picks, fitted_ref, tile_ref, *refs):
    *received, first_ref = refs[: len(refs) - (1 if other else len(picks)) + 1]
    out_refs = refs[len(received) :]
    size = first_ref.shape[0] // (len(picks) if other else 1)
    me = lax.axis_index("dp")
    turned = fitted_ref[...].astype(F32).T * (1.0 / math.sqrt(POINTS))
    turned = turned.astype(BF16)
    for n, j in enumerate(picks):
        first = owner(me, j, other) * size
        tile = tile_ref[:, pl.ds(pl.multiple_of(first, size), size)]
        out = jnp.dot(turned, tile, preferred_element_type=F32).T
        at = slice(n * size, (n + 1) * size)
        if other:
            first_ref[at, :] = out.astype(BF16)
        else:
            out_refs[n][...] = (out + received[0][at, :].astype(F32)).astype(BF16)


def back_call(fitted, tiles, other, picks, *received):
    rows, count = tiles.shape
    each = 1 if other else len(picks)
    return pl.pallas_call(
        functools.partial(back_kernel, other, picks),
        in_specs=[VMEM] * (2 + len(received)),
        out_specs=[VMEM] * each,
        out_shape=[pltpu.VMEM((len(picks) * count // 8 // each, WIDTH), BF16)] * each,
        compiler_params=pltpu.CompilerParams(vmem_limit_bytes=30 * 2**20),
        name="back_tiles",
    )(on_chip(fitted), on_chip(tiles), *[on_chip(r) for r in received])


def sum_kernel(in_ref, out_ref):
    total = in_ref[0].astype(F32)
    for k in range(1, in_ref.shape[0]):
        total += in_ref[k].astype(F32)
    total = total.astype(BF16)
    for k in range(in_ref.shape[0]):
        out_ref[k] = total


def sum_call(pieces):
    return pl.pallas_call(
        sum_kernel,
        in_specs=[VMEM],
        out_specs=VMEM,
        out_shape=pltpu.VMEM(pieces.shape, BF16),
        compiler_params=pltpu.CompilerParams(vmem_limit_bytes=4 * 2**20),
        name="sum_pieces",
    )(on_chip(pieces))


def add_kernel(a_ref, b_ref, out_ref):
    out_ref[...] = (a_ref[...].astype(F32) + b_ref[...].astype(F32)).astype(BF16)


def add_call(a, b):
    return pl.pallas_call(
        add_kernel,
        in_specs=[VMEM, VMEM],
        out_specs=VMEM,
        out_shape=pltpu.VMEM(a.shape, BF16),
        compiler_params=pltpu.CompilerParams(vmem_limit_bytes=4 * 2**20),
        name="add_pieces",
    )(on_chip(a), on_chip(b))


def begin_kernel(own_ref, along_ref, aside_ref, out_ref):
    own = jnp.where((lax.axis_index("dp") & 1) == 0, own_ref[...].astype(F32), 0.0)
    out_ref[...] = own + along_ref[...].astype(F32) + aside_ref[...].astype(F32)


def finish_kernel(begun_ref, begun_other_ref, last_ref, last_other_ref, out_ref):
    total = begun_ref[...] + begun_other_ref[...]
    total += last_ref[...].astype(F32) + last_other_ref[...].astype(F32)
    out_ref[...] = total.astype(BF16)


def gather_call(kernel, *pieces):
    return pl.pallas_call(
        kernel,
        in_specs=[VMEM] * len(pieces),
        out_specs=VMEM,
        out_shape=pltpu.VMEM(pieces[0].shape, F32 if kernel is begin_kernel else BF16),
        compiler_params=pltpu.CompilerParams(vmem_limit_bytes=4 * 2**20),
        name="sum_chips",
    )(*[on_chip(p) for p in pieces])


def widen_kernel(picks, *refs):
    *parts, out_ref, wide_ref, sems = refs
    me = lax.axis_index("dp")
    block = parts[0].shape[0]
    copies = []
    for n, (other, j, choice) in enumerate(picks):
        if choice[0] == choice[1]:
            wide_ref[n] = parts[choice[0]][...].astype(F32)
        else:
            zero = parts[choice[0]][...].astype(F32)
            one = parts[choice[1]][...].astype(F32)
            wide_ref[n] = jnp.where((me & 1) == other, zero, one)
        at = pl.ds(pl.multiple_of(owner(me, j, other) * block, block), block)
        copies.append(pltpu.make_async_copy(wide_ref.at[n], out_ref.at[at, :], sems.at[n]))
        copies[-1].start()
    for copy in copies:
        copy.wait()


def widen_call(parts, picks, base=None):
    block = parts[0].shape[0]
    more = [] if base is None else [base]
    count = len(parts)

    def kernel(*refs):
        widen_kernel(picks, *refs[:count], *refs[count + len(more) :])

    hbm = pl.BlockSpec(memory_space=pl.ANY)
    return pl.pallas_call(
        kernel,
        in_specs=[VMEM] * count + [hbm] * len(more),
        out_specs=hbm,
        out_shape=jax.ShapeDtypeStruct((8 * block, WIDTH), F32),
        input_output_aliases={count: 0} if more else {},
        scratch_shapes=[pltpu.VMEM((len(picks), block, WIDTH), F32), pltpu.SemaphoreType.DMA((len(picks),))],
        compiler_params=pltpu.CompilerParams(vmem_limit_bytes=4 * 2**20),
        name="widen",
    )(*[on_chip(p) for p in parts], *more)


def per_device(points, centers, direction):
    rows, count = points.shape[0], centers.shape[0]
    groups = lax.axis_size("center")
    swap = [(i, i ^ 1) for i in range(16)]

    tiles, partial_fit = fit_call(in_hbm(points), in_hbm(centers), in_hbm(direction))
    part = rows // groups
    pieces = lax.all_to_all(partial_fit.reshape(groups, part, WIDTH), "center", 0, 0)
    fitted = lax.all_to_all(sum_call(pieces), "center", 0, 0).reshape(rows, WIDTH)

    sends = {}
    halves = ((0, 2), (1, 3))
    received = [lax.ppermute(back_call(fitted, tiles, 1, picks)[0], "dp", swap) for picks in halves]
    for picks, r in zip(halves, received):
        sends.update(zip(picks, back_call(fitted, tiles, 0, picks, r)))
    hops = [tuple(row[j] for row in OFFSETS) for j in range(SETS)]
    relay = exchange(sends[0], RELAY)
    along = exchange(sends[2], hops[2])
    aside = exchange(sends[3], hops[3])
    relayed = add_call(sends[1], relay)
    begun = gather_call(begin_kernel, sends[3], along, aside)
    last = exchange(relayed, hops[1])
    full = gather_call(finish_kernel, begun, lax.ppermute(begun, "dp", swap), last, lax.ppermute(last, "dp", swap))
    pieces = [exchange(full, h) for h in hops[1:]]
    pieces = [exchange(pieces[0], RELAY)] + pieces
    others = [None] + [lax.ppermute(p, "dp", swap) for p in pieces[1:]]

    def write(out, *picks):
        parts, chosen = [full], []
        for other, j in picks:
            parts.append((others if other else pieces)[j])
            chosen.append((other, j, (0 if j == 3 else len(parts) - 1, len(parts) - 1)))
        return widen_call(parts, chosen, out)

    out = write(None, (0, 1), (0, 3), (1, 1))
    pieces[0], out = lax.optimization_barrier((pieces[0], out))
    others[0] = lax.ppermute(pieces[0], "dp", swap)
    out = write(out, (0, 2), (1, 3), (1, 2), (0, 0))
    return write(out, (1, 0))


def solution(mesh):
    return jax.shard_map(
        per_device,
        mesh=mesh,
        in_specs=(P("dp", None), P("center", None), P("center", None)),
        out_specs=P("center", None),
        check_vma=False,
    )
```
